32 devices in a mesh: dp: 4 (over z), seq: 8 (over y, x, core).
Axes of the slice: x: 2, y: 2, z: 4, core: 2. Of those that a mesh axis runs over, the one named last changes fastest.
Arguments:
- queries: bfloat16 [4, 1024, 12288], P('dp', 'seq'), may hold values from -8 to 8
- keys_in: bfloat16 [4, 1024, 768], P('dp', 'seq'), may hold values from -8 to 8
- values_in: bfloat16 [4, 1024, 512], P('dp', 'seq'), may hold values from -6 to 6
- gate_cmp: float32 [4, 1024, 64], P('dp', 'seq'), may hold values from 0.05 to 0.95
- gate_win: float32 [4, 1024, 64], P('dp', 'seq'), may hold values from 0.05 to 0.95
- cotangent: bfloat16 [4, 1024, 8192], P('dp', 'seq'), may hold values from -6 to 6
- compress_key: bfloat16 [6144, 192], replicated, may hold values from -1 to 1
- compress_value: bfloat16 [4096, 128], replicated, may hold values from -0.09375 to 0.09375
Outputs:
- attended: bfloat16 [4, 1024, 8192], P('dp', 'seq')
- grad_query: bfloat16 [4, 1024, 12288], P('dp', 'seq')
- grad_key: bfloat16 [4, 1024, 768], P('dp', 'seq')
- grad_value: bfloat16 [4, 1024, 512], P('dp', 'seq')
- grad_gate_cmp: float32 [4, 1024, 64], P('dp', 'seq')
- grad_gate_win: float32 [4, 1024, 64], P('dp', 'seq')
- grad_compress_key: float32 [6144, 192], P('seq')
- grad_compress_value: float32 [4096, 128], P('seq')
The draws below stay inside these ranges and needn't reach their ends.
All inputs are finite; a program needn't handle non-finite values.
Results may differ from the reference program's by a relative error of at most 0.023.
Values may be sent and summed in bfloat16 or wider, within the bound.
A program may use at most 192 MiB of HBM per device.

```python
import math
import jax
import jax.numpy as jnp
from jax import lax

H = 64
G = 4
DH = 192
DV = 128
BLK = 32
STRIDE = 16
WIN = 512
TOK_DEV = 128
SEQ = 1024
BATCH = 4


def draw_queries(key, part):
    base_draw = jax.random.truncated_normal(jax.random.fold_in(key, 21), -6.0, 6.0, (BATCH, SEQ, H * DH), jnp.float32)
    return base_draw.astype(jnp.bfloat16)


def draw_keys_in(key, part):
    base_draw = jax.random.truncated_normal(jax.random.fold_in(key, 22), -6.0, 6.0, (BATCH, SEQ, G * DH), jnp.float32)
    return base_draw.astype(jnp.bfloat16)


def draw_compress_key(key, part):
    base_draw = jax.random.truncated_normal(jax.random.fold_in(key, 23), -6.0, 6.0, (BLK * DH, DH), jnp.float32) / math.sqrt(BLK * DH)
    return base_draw.astype(jnp.bfloat16)


def levels(rng, shape, cuts, low, largest):
    def one(axis_at, shards_of):
        draws = jax.random.uniform(jax.random.fold_in(jax.random.fold_in(rng, 6), axis_at), (shards_of,), jnp.float32, low / len(cuts), largest / len(cuts))
        return jnp.repeat(jnp.exp(draws), shape[axis_at] // shards_of).reshape((-1,) + (1,) * (len(shape) - axis_at - 1))

    gain = one(*cuts[0])
    for cut in cuts[1:]:
        gain = gain * one(*cut)
    return gain


def scatter_about(stream_key, dims, scale, limit, split=(), kind=jnp.bfloat16):
    factor_of = levels(stream_key, dims, split, -0.22, 0.18) if split else 1.0
    array = jax.random.normal(stream_key, dims, jnp.float32) * scale * factor_of
    return jnp.minimum(jnp.maximum(array, -limit), limit).astype(kind)


def setup_inputs(seed: int = 0) -> dict:
    keys = jax.random.split(jax.random.key(seed), 9)
    return {
        "queries": draw_queries(jax.random.fold_in(keys[8], 71), 0),
        "keys_in": draw_keys_in(jax.random.fold_in(keys[8], 71), 0),
        "values_in": scatter_about(keys[2], (BATCH, SEQ, G * DV), 1.0, 6.0, ((0, 4), (1, 8))),
        "gate_cmp": jnp.clip(0.05 + 0.9 * jax.random.uniform(keys[3], (BATCH, SEQ, H), jnp.float32) ** levels(keys[3], (BATCH, SEQ, H), ((0, 4), (1, 8)), -0.2, 0.2), 0.05, 0.95),
        "gate_win": jnp.clip(0.05 + 0.9 * jax.random.uniform(keys[4], (BATCH, SEQ, H), jnp.float32) ** levels(keys[4], (BATCH, SEQ, H), ((0, 4), (1, 8)), -0.2, 0.2), 0.05, 0.95),
        "cotangent": scatter_about(keys[5], (BATCH, SEQ, H * DV), 1.0, 6.0, ((0, 4), (1, 8))),
        "compress_key": draw_compress_key(jax.random.fold_in(keys[8], 71), 0),
        "compress_value": scatter_about(keys[7], (BLK * DV, DV), (BLK * DV) ** -0.5, 0.09375),
    }


def attend(query_b, keys_b, values_b, valid, gate_vals, cotangent_b):
    scaling = 1.0 / math.sqrt(query_b.shape[-1])
    query_f = query_b.astype(jnp.float32)
    keys_f = keys_b.astype(jnp.float32)
    values_f = values_b.astype(jnp.float32)
    scores = jnp.einsum('tgcd,kgd->tgck', query_f, keys_f) * scaling
    scores = jnp.where(valid[:, None, None, :], scores, -1e+30)
    row_max = lax.optimization_barrier(jnp.max(scores, axis=-1, keepdims=True))
    exponent = jnp.exp(scores - row_max)
    softmax_w = exponent / lax.optimization_barrier(jnp.sum(exponent, axis=-1, keepdims=True))
    softmax_b = softmax_w.astype(jnp.bfloat16).astype(jnp.float32)
    branch_out = jnp.einsum('tgck,kgd->tgcd', softmax_b, values_f)
    cotangent_f = cotangent_b.astype(jnp.float32)
    grad_gate = lax.optimization_barrier(jnp.sum(cotangent_f * branch_out, axis=-1))
    grad_out = (gate_vals[..., None] * cotangent_f).astype(jnp.bfloat16).astype(jnp.float32)
    grad_v = jnp.einsum('tgck,tgcd->kgd', softmax_b, grad_out)
    grad_prob = jnp.einsum('tgcd,kgd->tgck', grad_out, values_f)
    row_delta = lax.optimization_barrier(jnp.sum(grad_out * branch_out, axis=-1, keepdims=True))
    grad_score = (softmax_w * (grad_prob - row_delta) * scaling).astype(jnp.bfloat16).astype(jnp.float32)
    grad_q = jnp.einsum('tgck,kgd->tgcd', grad_score, keys_f)
    grad_k = jnp.einsum('tgck,tgcd->kgd', grad_score, query_f)
    return (branch_out, grad_gate, grad_q, grad_k, grad_v)

def compress(keys_b, weight):
    width = keys_b.shape[1]
    head_dim = weight.shape[1]
    groups = width // head_dim
    padded = jnp.concatenate([jnp.zeros((BLK, width), jnp.bfloat16), keys_b[:SEQ - STRIDE]], axis=0)
    halves = padded.reshape(-1, STRIDE, groups, head_dim)
    blocks = jnp.concatenate([halves[:-1], halves[1:]], axis=1)
    weight_cube = weight.reshape(BLK, head_dim, head_dim).astype(jnp.float32)
    compressed = jnp.einsum('bpgd,pde->bge', blocks.astype(jnp.float32), weight_cube).astype(jnp.bfloat16)
    return (blocks, compressed)

def compress_back(blocks, weight, grad_blocks):
    groups = blocks.shape[2]
    head_dim = weight.shape[1]
    weight_cube = weight.reshape(BLK, head_dim, head_dim).astype(jnp.float32)
    grad_round = grad_blocks.astype(jnp.bfloat16).astype(jnp.float32)
    grad_slabs = jnp.einsum('bge,pde->bpgd', grad_round, weight_cube)
    grad_weight = jnp.einsum('bpgd,bge->pde', blocks.astype(jnp.float32), grad_round).reshape(BLK * head_dim, head_dim)
    zero_half = jnp.zeros((1, STRIDE, groups, head_dim), jnp.float32)
    grad_halves = jnp.concatenate([grad_slabs[:, :STRIDE], zero_half], axis=0) + jnp.concatenate([zero_half, grad_slabs[:, STRIDE:]], axis=0)
    grad_padded = grad_halves.reshape(-1, groups * head_dim)
    grad_tokens = jnp.concatenate([grad_padded[BLK:], jnp.zeros((STRIDE, groups * head_dim), jnp.float32)], axis=0)
    return (grad_tokens, grad_weight)

def one_sequence(queries, keys_in, values_in, gate_cmp, gate_win, cotangent, compress_key, compress_value):
    kv_width = keys_in.shape[1]
    value_width = values_in.shape[1]
    groups = kv_width // DH
    per_group = H // groups
    reach_shards = (WIN + TOK_DEV - 1) // TOK_DEV
    lead_count = reach_shards * TOK_DEV
    key_count = lead_count + TOK_DEV
    key_blocks, cmp_keys = compress(keys_in, compress_key)
    value_blocks, cmp_values = compress(values_in, compress_value)
    block_count = cmp_keys.shape[0]
    keys_wide = jnp.concatenate([jnp.zeros((lead_count, kv_width), jnp.bfloat16), keys_in], axis=0).reshape(-1, groups, DH)
    values_wide = jnp.concatenate([jnp.zeros((lead_count, value_width), jnp.bfloat16), values_in], axis=0).reshape(-1, groups, DV)

    def step_block(totals, block_index):
        grad_kw, grad_vw, grad_ck, grad_cv = totals
        first_row = block_index * TOK_DEV
        query_b = lax.dynamic_slice_in_dim(queries, first_row, TOK_DEV, 0).reshape(TOK_DEV, groups, per_group, DH)
        cotangent_b = lax.dynamic_slice_in_dim(cotangent, first_row, TOK_DEV, 0).reshape(TOK_DEV, groups, per_group, DV)
        gate_c = lax.dynamic_slice_in_dim(gate_cmp, first_row, TOK_DEV, 0).reshape(TOK_DEV, groups, per_group)
        gate_w = lax.dynamic_slice_in_dim(gate_win, first_row, TOK_DEV, 0).reshape(TOK_DEV, groups, per_group)
        window_k = lax.dynamic_slice_in_dim(keys_wide, first_row, key_count, 0)
        window_v = lax.dynamic_slice_in_dim(values_wide, first_row, key_count, 0)
        query_pos = first_row + jnp.arange(TOK_DEV, dtype=jnp.int32)
        key_pos = first_row - lead_count + jnp.arange(key_count, dtype=jnp.int32)
        distance = query_pos[:, None] - key_pos[None, :]
        window_mask = (key_pos[None, :] >= 0) & (distance >= 0) & (distance < WIN)
        causal_mask = STRIDE * jnp.arange(block_count, dtype=jnp.int32)[None, :] <= query_pos[:, None] + 1
        out_cmp, gate_grad_c, grad_q_c, grad_k_c, grad_v_c = attend(query_b, cmp_keys, cmp_values, causal_mask, gate_c, cotangent_b)
        out_win, gate_grad_w, grad_q_w, grad_k_w, grad_v_w = attend(query_b, window_k, window_v, window_mask, gate_w, cotangent_b)
        out_block = (gate_c[..., None] * out_cmp + gate_w[..., None] * out_win).astype(jnp.bfloat16).reshape(TOK_DEV, -1)
        grad_q_block = (grad_q_c + grad_q_w).astype(jnp.bfloat16).reshape(TOK_DEV, -1)
        grad_kw = lax.dynamic_update_slice_in_dim(grad_kw, lax.dynamic_slice_in_dim(grad_kw, first_row, key_count, 0) + grad_k_w.reshape(key_count, kv_width), first_row, 0)
        grad_vw = lax.dynamic_update_slice_in_dim(grad_vw, lax.dynamic_slice_in_dim(grad_vw, first_row, key_count, 0) + grad_v_w.reshape(key_count, value_width), first_row, 0)
        totals = (grad_kw, grad_vw, grad_ck + grad_k_c, grad_cv + grad_v_c)
        return (totals, (out_block, grad_q_block, gate_grad_c.reshape(TOK_DEV, -1), gate_grad_w.reshape(TOK_DEV, -1)))
    start_totals = (jnp.zeros((lead_count + SEQ, kv_width), jnp.float32), jnp.zeros((lead_count + SEQ, value_width), jnp.float32), jnp.zeros((block_count, groups, DH), jnp.float32), jnp.zeros((block_count, groups, DV), jnp.float32))
    totals, stacked = lax.scan(step_block, start_totals, jnp.arange(SEQ // TOK_DEV, dtype=jnp.int32))
    grad_kw, grad_vw, grad_ck, grad_cv = totals
    grad_k_cmp, grad_wk = compress_back(key_blocks, compress_key, grad_ck)
    grad_v_cmp, grad_wv = compress_back(value_blocks, compress_value, grad_cv)
    grad_key = (grad_kw[lead_count:] + grad_k_cmp).astype(jnp.bfloat16)
    grad_value = (grad_vw[lead_count:] + grad_v_cmp).astype(jnp.bfloat16)
    attended = stacked[0].reshape(SEQ, -1)
    grad_query = stacked[1].reshape(SEQ, -1)
    return (attended, grad_query, grad_key, grad_value, stacked[2].reshape(SEQ, -1), stacked[3].reshape(SEQ, -1), grad_wk, grad_wv)

def sum_list(arrays):
    total = arrays[0]
    for other in arrays[1:]:
        total = total + other
    return total

def reference(queries, keys_in, values_in, gate_cmp, gate_win, cotangent, compress_key, compress_value):
    results = []
    for seq_index in range(BATCH):
        results.append(one_sequence(queries[seq_index], keys_in[seq_index], values_in[seq_index], gate_cmp[seq_index], gate_win[seq_index], cotangent[seq_index], compress_key, compress_value))
    stacked = [jnp.stack([item[slot] for item in results]) for slot in range(6)]
    grad_wk = sum_list([item[6] for item in results])
    grad_wv = sum_list([item[7] for item in results])
    return (stacked[0], stacked[1], stacked[2], stacked[3], stacked[4], stacked[5], grad_wk, grad_wv)
```

```python
import functools
import math

import jax
import jax.numpy as jnp
from jax import lax
from jax.experimental import pallas as pl
from jax.experimental.pallas import tpu as pltpu
from jax.sharding import PartitionSpec as P

BLK = 32
STRIDE = 16
WIN = 512
NEG = -1e30
F32 = jnp.float32
BF16 = jnp.bfloat16
VLIM = 56 * 1024 * 1024


def mm(a, b, ca, cb):
    return lax.dot_general(a, b, (((ca,), (cb,)), ((), ())), preferred_element_type=F32)


def full(memory=pltpu.VMEM):
    return pl.BlockSpec(memory_space=memory)


def up128(n):
    return (n + 127) // 128 * 128


def stack_groups(rows, groups, width):
    return jnp.concatenate([rows[:, g * width : (g + 1) * width] for g in range(groups)], axis=0)


def fill_padded(pad_ref, kv_ref):
    for i in range(pad_ref.shape[0]):
        pad_ref[i, 0:BLK, :] = jnp.zeros((BLK, 128), F32)
        pad_ref[i, BLK:, :] = kv_ref[:, 128 * i : 128 * (i + 1)].astype(F32)


def every_stride(pad_ref, p, nb):
    tiles = [pad_ref[i, pl.ds(p, nb, stride=STRIDE), :] for i in range(pad_ref.shape[0])]
    return jnp.concatenate(tiles, axis=1)


def prep_kernel(dims, kv_ref, wk_ref, wv_ref, k_ref, kt_ref, v_ref, vt_ref, pad_ref):
    groups, dk, dv, rows, reach, nb = dims
    kw = groups * dk
    index = lax.axis_index("seq")
    win = (reach + 1) * rows
    fill_padded(pad_ref, kv_ref)
    for c in range(reach + 1):
        shard = jnp.maximum(index - reach + c, 0)
        chunk = kv_ref[pl.ds(pl.multiple_of(shard * rows, rows), rows), :]
        for g in range(groups):
            k_ref[g, c * rows : (c + 1) * rows, :] = chunk[:, g * dk : (g + 1) * dk]
            v_ref[g, c * rows : (c + 1) * rows, :] = chunk[:, kw + g * dv : kw + (g + 1) * dv]
    ck = jnp.zeros((groups * nb, dk), F32)
    cv = jnp.zeros((groups * nb, dv), F32)
    for p in range(BLK):
        at = every_stride(pad_ref, p, nb).astype(BF16)
        ck += mm(stack_groups(at[:, :kw], groups, dk), wk_ref[p * dk : (p + 1) * dk, :], 1, 0)
        cv += mm(stack_groups(at[:, kw:], groups, dv), wv_ref[p * dv : (p + 1) * dv, :], 1, 0)
    for g in range(groups):
        k_ref[g, win:, :] = ck[g * nb : (g + 1) * nb].astype(BF16)
        v_ref[g, win:, :] = cv[g * nb : (g + 1) * nb].astype(BF16)
        kt_ref[g] = k_ref[g].T
        vt_ref[g] = v_ref[g].T


def prep(kv_all, wk, wv, groups, rows, reach):
    dk, dv = wk.shape[1], wv.shape[1]
    nb = kv_all.shape[0] // STRIDE
    total = (reach + 1) * rows + nb
    dims = (groups, dk, dv, rows, reach, nb)
    sds = lambda *s: jax.ShapeDtypeStruct(s, BF16)
    return pl.pallas_call(
        functools.partial(prep_kernel, dims),
        out_shape=(
            sds(groups, total, dk),
            sds(groups, dk, total),
            sds(groups, total, dv),
            sds(groups, dv, total),
        ),
        in_specs=[full()] * 3,
        out_specs=(full(),) * 4,
        scratch_shapes=[pltpu.VMEM((kv_all.shape[1] // 128, kv_all.shape[0] + BLK, 128), F32)],
        compiler_params=pltpu.CompilerParams(vmem_limit_bytes=VLIM),
    )(kv_all, wk, wv)


def back_kernel(dims, gc_ref, kv_ref, wk_ref, wv_ref, gwk_ref, gwv_ref, own_ref, pad_ref, gf_ref, own_s):
    groups, dk, dv, rows, nb, off = dims
    kw = groups * dk
    index = lax.axis_index("seq")
    per = gwk_ref.shape[0] // dk
    blocks = rows // STRIDE
    fill_padded(pad_ref, kv_ref)
    gk = gc_ref[:, :dk]
    gv = gc_ref[:, off : off + dv]
    for i in range(per):
        at = every_stride(pad_ref, index * per + i, nb)
        kst = stack_groups(at[:, :kw], groups, dk).T.astype(BF16)
        vst = stack_groups(at[:, kw:], groups, dv).T.astype(BF16)
        gwk_ref[i * dk : (i + 1) * dk, :] = mm(kst, gk, 1, 0).astype(BF16)
        gwv_ref[i * dv : (i + 1) * dv, :] = mm(vst, gv, 1, 0).astype(BF16)
    for g in range(groups):
        gf_ref[g, 0:nb, :] = gc_ref[g * nb : (g + 1) * nb, :].astype(F32)
        gf_ref[g, nb:, :] = jnp.zeros((gf_ref.shape[1] - nb, gf_ref.shape[2]), F32)
    base = pl.multiple_of(index * blocks, blocks)
    ahead = [gf_ref[g, pl.ds(base, blocks + 8), :] for g in range(groups)]
    near = jnp.concatenate([x[1 : blocks + 1] for x in ahead], axis=0)
    far = jnp.concatenate([x[2 : blocks + 2] for x in ahead], axis=0)
    near, far = near.astype(BF16), far.astype(BF16)
    for q in range(STRIDE):
        lo, hi = q, q + STRIDE
        k = mm(far[:, :dk], wk_ref[lo * dk : (lo + 1) * dk, :], 1, 1)
        k += mm(near[:, :dk], wk_ref[hi * dk : (hi + 1) * dk, :], 1, 1)
        v = mm(far[:, off : off + dv], wv_ref[lo * dv : (lo + 1) * dv, :], 1, 1)
        v += mm(near[:, off : off + dv], wv_ref[hi * dv : (hi + 1) * dv, :], 1, 1)
        parts = [k[g * blocks : (g + 1) * blocks] for g in range(groups)]
        parts += [v[g * blocks : (g + 1) * blocks] for g in range(groups)]
        row = jnp.concatenate(parts, axis=1)
        for i in range(own_s.shape[0]):
            own_s[i, pl.ds(q, blocks, stride=STRIDE), :] = row[:, 128 * i : 128 * (i + 1)]
    for i in range(own_s.shape[0]):
        own_ref[:, 128 * i : 128 * (i + 1)] = own_s[i]


def back(gc, kv_all, wk, wv, groups, rows, off, devices):
    dk, dv = wk.shape[1], wv.shape[1]
    nb = kv_all.shape[0] // STRIDE
    dims = (groups, dk, dv, rows, nb, off)
    return pl.pallas_call(
        functools.partial(back_kernel, dims),
        out_shape=(
            jax.ShapeDtypeStruct((wk.shape[0] // devices, dk), BF16),
            jax.ShapeDtypeStruct((wv.shape[0] // devices, dv), BF16),
            jax.ShapeDtypeStruct((rows, kv_all.shape[1]), F32),
        ),
        in_specs=[full()] * 4,
        out_specs=(full(),) * 3,
        scratch_shapes=[
            pltpu.VMEM((kv_all.shape[1] // 128, kv_all.shape[0] + BLK, 128), F32),
            pltpu.VMEM((groups, nb + 8, gc.shape[1]), F32),
            pltpu.VMEM((kv_all.shape[1] // 128, rows, 128), F32),
        ],
        compiler_params=pltpu.CompilerParams(vmem_limit_bytes=VLIM),
    )(gc, kv_all, wk, wv)


def bias_win(index, rows, reach):
    count = (reach + 1) * rows
    j = lax.broadcasted_iota(jnp.int32, (count, 2 * rows), 0) - reach * rows
    t = lax.broadcasted_iota(jnp.int32, (count, 2 * rows), 1)
    t = jnp.where(t >= rows, t - rows, t)
    ok = (j <= t) & (t - j < WIN) & (j + index * rows >= 0)
    return jnp.where(ok, 0.0, NEG).astype(F32)


def bias_cmp(index, rows, nb):
    b = lax.broadcasted_iota(jnp.int32, (nb, 2 * rows), 0)
    t = lax.broadcasted_iota(jnp.int32, (nb, 2 * rows), 1)
    t = jnp.where(t >= rows, t - rows, t)
    return jnp.where(STRIDE * b <= t + index * rows + 1, 0.0, NEG).astype(F32)


def branch(s, cp, bias, gate, scaling):
    s = s * (scaling * math.log2(math.e)) + bias
    e = jnp.exp2(s - jnp.max(s, axis=0, keepdims=True))
    inv = 1.0 / jnp.sum(e, axis=0, keepdims=True)
    gg = jnp.sum(e * cp, axis=0, keepdims=True) * inv
    w = (e * (gate * inv)).astype(BF16)
    gs = (e * (cp - gg) * (gate * (inv * scaling))).astype(BF16)
    return gg, w, gs


def load_pair(i, rows, dk, dv, q_ref, c_ref, qs, cs):
    base = 2 * i * rows
    both = q_ref[:, 2 * i * dk : 2 * (i + 1) * dk]
    qs[base : base + rows, :] = both[:, :dk]
    qs[base + rows : base + 2 * rows, :] = both[:, dk:]
    cs[base : base + rows, :] = c_ref[:, 2 * i * dv : (2 * i + 1) * dv]
    cs[base + rows : base + 2 * rows, :] = c_ref[:, (2 * i + 1) * dv : (2 * i + 2) * dv]
    return qs[base : base + 2 * rows, :], cs[base : base + 2 * rows, :]


def pair_gate(gate_t, first, i):
    return jnp.concatenate([gate_t[2 * i : 2 * i + 1, :], gate_t[2 * i + 1 : 2 * i + 2, :]], axis=1)


def cmp_kernel(dims, q_ref, c_ref, k_ref, v_ref, gate_ref, out_ref, bias, gate_s, qs, cs, ws, gss):
    rows, per, dk, dv, nb, off, reach = dims
    win = (reach + 1) * rows
    step = pl.program_id(0)

    @pl.when(step == 0)
    def _():
        bias[...] = bias_cmp(lax.axis_index("seq"), rows, nb)
        gate_s[...] = gate_ref[...].T

    gate_t = gate_s[pl.ds(pl.multiple_of(step * per, per), per), :]
    k = k_ref[0, win:, :]
    v = v_ref[0, win:, :]
    scaling = 1.0 / math.sqrt(dk)
    for i in range(per // 2):
        q2, c2 = load_pair(i, rows, dk, dv, q_ref, c_ref, qs, cs)
        gate = pair_gate(gate_t, 0, i)
        _, w, gs = branch(mm(k, q2, 1, 1), mm(v, c2, 1, 1), bias[...], gate, scaling)
        ws[:, 2 * i * rows : 2 * (i + 1) * rows] = w
        gss[:, 2 * i * rows : 2 * (i + 1) * rows] = gs
    out_ref[:, :dk] = mm(gss[...], qs[...], 1, 0).astype(BF16)
    if off > dk:
        out_ref[:, dk:off] = jnp.zeros((nb, off - dk), BF16)
    out_ref[:, off:] = mm(ws[...], cs[...], 1, 0).astype(BF16)


def cmp_grads(q, c, kall, vall, gate, groups, reach, nb, off):
    rows = q.shape[0]
    heads = gate.shape[1]
    per = heads // groups
    dk, dv, total = kall.shape[2], vall.shape[2], kall.shape[1]
    dims = (rows, per, dk, dv, nb, off, reach)
    return pl.pallas_call(
        functools.partial(cmp_kernel, dims),
        grid=(groups,),
        out_shape=jax.ShapeDtypeStruct((groups * nb, off + dv), BF16),
        in_specs=[
            pl.BlockSpec((rows, per * dk), lambda g: (0, g)),
            pl.BlockSpec((rows, per * dv), lambda g: (0, g)),
            pl.BlockSpec((1, total, dk), lambda g: (g, 0, 0)),
            pl.BlockSpec((1, total, dv), lambda g: (g, 0, 0)),
            pl.BlockSpec((rows, heads), lambda g: (0, 0)),
        ],
        out_specs=pl.BlockSpec((nb, off + dv), lambda g: (g, 0)),
        scratch_shapes=[
            pltpu.VMEM((nb, 2 * rows), F32),
            pltpu.VMEM((heads, rows), F32),
            pltpu.VMEM((per * rows, dk), BF16),
            pltpu.VMEM((per * rows, dv), BF16),
            pltpu.VMEM((nb, per * rows), BF16),
            pltpu.VMEM((nb, per * rows), BF16),
        ],
        compiler_params=pltpu.CompilerParams(vmem_limit_bytes=VLIM),
    )(q, c, kall, vall, gate)


def main_kernel(dims, alias, *refs):
    rows, hc, chunks, dk, dv, nb, off, reach, first = dims
    q_ref, c_ref, k_ref, kt_ref, v_ref, vt_ref, gc_ref, gw_ref = refs[:8]
    refs = refs[10:] if alias else refs[8:]
    att_ref, gq_ref, send_ref, own_ref, ggc_ref, ggw_ref = refs[:6]
    bias, gct, gwt, ggct, ggwt, qs, cs, ws, gss, acck, accv = refs[6:]
    win = (reach + 1) * rows
    lead = reach * rows
    g, part = pl.program_id(0), pl.program_id(1)
    step = g * chunks + part

    @pl.when(step == 0)
    def _():
        index = lax.axis_index("seq")
        bias[:win, :] = bias_win(index, rows, reach)
        bias[win:, :] = bias_cmp(index, rows, nb)
        gct[...] = gc_ref[...].T
        gwt[...] = gw_ref[...].T

    row0 = pl.multiple_of(step * hc, hc)
    head0 = pl.multiple_of(first * hc * chunks + step * hc, hc)
    gate_c = gct[pl.ds(head0, hc), :]
    gate_w = gwt[pl.ds(head0, hc), :]
    scaling = 1.0 / math.sqrt(dk)
    rows_c, rows_w = [], []
    for i in range(hc // 2):
        q2, c2 = load_pair(i, rows, dk, dv, q_ref, c_ref, qs, cs)
        s = mm(k_ref[0], q2, 1, 1)
        cp = mm(v_ref[0], c2, 1, 1)
        gg_w, w_w, gs_w = branch(s[:win], cp[:win], bias[:win, :], pair_gate(gate_w, 0, i), scaling)
        gg_c, w_c, gs_c = branch(s[win:], cp[win:], bias[win:, :], pair_gate(gate_c, 0, i), scaling)
        cols = slice(2 * i * rows, 2 * (i + 1) * rows)
        ws[:win, cols] = w_w
        ws[win:, cols] = w_c
        gss[:win, cols] = gs_w
        gss[win:, cols] = gs_c
        rows_w += [gg_w[:, :rows], gg_w[:, rows:]]
        rows_c += [gg_c[:, :rows], gg_c[:, rows:]]
        att = mm(vt_ref[0], ws[:, cols], 1, 0)
        gq = mm(kt_ref[0], gss[:, cols], 1, 0)
        att = jnp.concatenate([att[:, :rows], att[:, rows:]], axis=0)
        gq = jnp.concatenate([gq[:, :rows], gq[:, rows:]], axis=0)
        att_ref[:, 2 * i * dv : 2 * (i + 1) * dv] = att.T.astype(BF16)
        gq_ref[:, 2 * i * dk : 2 * (i + 1) * dk] = gq.T.astype(BF16)
    ggct[pl.ds(row0, hc), :] = jnp.concatenate(rows_c, axis=0)
    ggwt[pl.ds(row0, hc), :] = jnp.concatenate(rows_w, axis=0)
    gk = mm(gss[:win, :], qs[...], 1, 0)
    gv = mm(ws[:win, :], cs[...], 1, 0)

    @pl.when(part == 0)
    def _():
        acck[...] = gk
        accv[...] = gv

    @pl.when(part > 0)
    def _():
        acck[...] += gk
        accv[...] += gv

    @pl.when(part == chunks - 1)
    def _():
        send_ref[0, :, :dk] = acck[:lead, :].astype(BF16)
        send_ref[0, :, off:] = accv[:lead, :].astype(BF16)
        own_ref[0, :, :dk] = acck[lead:, :]
        own_ref[0, :, off:] = accv[lead:, :]
        if off > dk:
            send_ref[0, :, dk:off] = jnp.zeros((lead, off - dk), BF16)
            own_ref[0, :, dk:off] = jnp.zeros((rows, off - dk), F32)
        ggc_ref[...] = ggct[...].T
        ggw_ref[...] = ggwt[...].T


def attend(q, c, prepped, gate_c, gate_w, first, count, groups, reach, nb, off, into):
    kall, kt, vall, vt = prepped
    rows = q.shape[0]
    heads = gate_c.shape[1]
    per = heads // groups
    hc = 8
    chunks = per // hc
    dk, dv, total = kall.shape[2], vall.shape[2], kall.shape[1]
    win = (reach + 1) * rows
    dims = (rows, hc, chunks, dk, dv, nb, off, reach, first)
    col = lambda g, p: (0, (first + g) * chunks + p)
    grp = lambda g, p: (first + g, 0, 0)
    whole = lambda g, p: (0, 0)
    sds = jax.ShapeDtypeStruct
    in_specs = [
        pl.BlockSpec((rows, hc * dk), col),
        pl.BlockSpec((rows, hc * dv), col),
        pl.BlockSpec((1, total, dk), grp),
        pl.BlockSpec((1, dk, total), grp),
        pl.BlockSpec((1, total, dv), grp),
        pl.BlockSpec((1, dv, total), grp),
        pl.BlockSpec((rows, heads), whole),
        pl.BlockSpec((rows, heads), whole),
    ]
    args = [q, c, kall, kt, vall, vt, gate_c, gate_w]
    aliases = {}
    if into is not None:
        in_specs += [pl.BlockSpec(memory_space=pl.ANY)] * 2
        args += list(into)
        aliases = {8: 0, 9: 1}
    flops = 2 * 2 * 3 * rows * per * count * total * (dk + dv)
    return pl.pallas_call(
        functools.partial(main_kernel, dims, into is not None),
        grid=(count, chunks),
        out_shape=(
            sds((rows, heads * dv), BF16),
            sds((rows, heads * dk), BF16),
            sds((count, reach * rows, off + dv), BF16),
            sds((count, rows, off + dv), F32),
            sds((rows, per * count), F32),
            sds((rows, per * count), F32),
        ),
        in_specs=in_specs,
        out_specs=(
            pl.BlockSpec((rows, hc * dv), col),
            pl.BlockSpec((rows, hc * dk), col),
            pl.BlockSpec((1, reach * rows, off + dv), lambda g, p: (g, 0, 0)),
            pl.BlockSpec((1, rows, off + dv), lambda g, p: (g, 0, 0)),
            pl.BlockSpec((rows, per * count), whole),
            pl.BlockSpec((rows, per * count), whole),
        ),
        scratch_shapes=[
            pltpu.VMEM((total, 2 * rows), F32),
            pltpu.VMEM((heads, rows), F32),
            pltpu.VMEM((heads, rows), F32),
            pltpu.VMEM((per * count, rows), F32),
            pltpu.VMEM((per * count, rows), F32),
            pltpu.VMEM((hc * rows, dk), BF16),
            pltpu.VMEM((hc * rows, dv), BF16),
            pltpu.VMEM((total, hc * rows), BF16),
            pltpu.VMEM((total, hc * rows), BF16),
            pltpu.VMEM((win, dk), F32),
            pltpu.VMEM((win, dv), F32),
        ],
        input_output_aliases=aliases,
        cost_estimate=pl.CostEstimate(flops=4 * flops, bytes_accessed=rows * heads * (dk + dv) * 4, transcendentals=0),
        compiler_params=pltpu.CompilerParams(vmem_limit_bytes=VLIM),
    )(*args)


def finish_kernel(dims, cmp_ref, *refs):
    groups, dk, dv, off, halves = dims
    k_ref, v_ref = refs[-2:]
    ins = refs[:-2]
    kw = groups * dk
    each = groups // halves
    per_half = len(ins) // halves
    ks, vs = [], []
    for half in range(halves):
        mine = ins[half * per_half : (half + 1) * per_half]
        for g in range(each):
            total = mine[0][g]
            for ref in mine[1:]:
                total = total + ref[g].astype(F32)
            ks.append(total[:, :dk])
            vs.append(total[:, off:])
    k_ref[...] = (jnp.concatenate(ks, axis=1) + cmp_ref[:, :kw]).astype(BF16)
    v_ref[...] = (jnp.concatenate(vs, axis=1) + cmp_ref[:, kw:]).astype(BF16)


def finish(own_cmp, parts, groups, dk, dv, off, halves):
    rows = own_cmp.shape[0]
    return pl.pallas_call(
        functools.partial(finish_kernel, (groups, dk, dv, off, halves)),
        out_shape=(
            jax.ShapeDtypeStruct((rows, groups * dk), BF16),
            jax.ShapeDtypeStruct((rows, groups * dv), BF16),
        ),
        in_specs=[full()] * (1 + len(parts)),
        out_specs=(full(),) * 2,
        compiler_params=pltpu.CompilerParams(vmem_limit_bytes=VLIM),
    )(own_cmp, *parts)


def send_back(send, rows, reach):
    devices = lax.axis_size("seq")
    got = []
    for distance in range(1, reach + 1):
        at = (reach - distance) * rows
        pairs = [(i, i - distance) for i in range(devices) if i - distance >= 0]
        got.append(lax.ppermute(send[:, at : at + rows], "seq", pairs))
    return got


def on_device(queries, keys_in, values_in, gate_cmp, gate_win, cotangent, compress_key, compress_value):
    rows = queries.shape[1]
    dk, dv = compress_key.shape[1], compress_value.shape[1]
    groups = keys_in.shape[2] // dk
    devices = lax.axis_size("seq")
    reach = (WIN + rows - 1) // rows
    off = up128(dk)
    q, c = queries[0], cotangent[0]
    gc, gw = gate_cmp[0], gate_win[0]
    kv = jnp.concatenate([keys_in[0], values_in[0]], axis=1)
    kv_all = lax.all_gather(kv, "seq", axis=0, tiled=True)
    nb = kv_all.shape[0] // STRIDE
    prepped = prep(kv_all, compress_key, compress_value, groups, rows, reach)
    part = cmp_grads(q, c, prepped[0], prepped[2], gc, groups, reach, nb, off)
    half = groups // 2
    total = lax.psum(part, "seq")
    a = attend(q, c, prepped, gc, gw, 0, half, groups, reach, nb, off, None)
    back_a = send_back(a[2], rows, reach)
    total, att, gq = lax.optimization_barrier((total, a[0], a[1]))
    gwk, gwv, own_cmp = back(total, kv_all, compress_key, compress_value, groups, rows, off, devices)
    gwk_sum, gwv_sum = lax.psum(gwk, "dp"), lax.psum(gwv, "dp")
    att, gq, own_cmp = lax.optimization_barrier((att, gq, own_cmp))
    b = attend(q, c, prepped, gc, gw, half, groups - half, groups, reach, nb, off, (att, gq))
    back_b = send_back(b[2], rows, reach)
    gk, gv = finish(own_cmp, [a[3], *back_a, b[3], *back_b], groups, dk, dv, off, 2)
    return (
        b[0][None],
        b[1][None],
        gk[None],
        gv[None],
        jnp.concatenate([a[4], b[4]], axis=1)[None],
        jnp.concatenate([a[5], b[5]], axis=1)[None],
        gwk_sum.astype(F32),
        gwv_sum.astype(F32),
    )


def solution(mesh):
    tokens = P("dp", "seq", None)
    in_specs = (tokens,) * 6 + (P(), P())
    out_specs = (tokens,) * 6 + (P("seq", None), P("seq", None))
    return jax.shard_map(on_device, mesh=mesh, in_specs=in_specs, out_specs=out_specs, check_vma=False)
```

```python
import functools
import math

import jax
import jax.numpy as jnp
from jax import lax
from jax.experimental import pallas as pl
from jax.experimental.pallas import tpu as pltpu
from jax.sharding import PartitionSpec as P

BLK = 32
STRIDE = 16
WIN = 512
NEG = -1e30
F32 = jnp.float32
BF16 = jnp.bfloat16
VLIM = 56 * 1024 * 1024


def mm(a, b, ca, cb):
    return lax.dot_general(a, b, (((ca,), (cb,)), ((), ())), preferred_element_type=F32)


def full(memory=pltpu.VMEM):
    return pl.BlockSpec(memory_space=memory)


def up128(n):
    return (n + 127) // 128 * 128


def stack_groups(rows, groups, width):
    return jnp.concatenate([rows[:, g * width : (g + 1) * width] for g in range(groups)], axis=0)


def fill_padded(pad_ref, kv_ref):
    for i in range(pad_ref.shape[0]):
        pad_ref[i, 0:BLK, :] = jnp.zeros((BLK, 128), F32)
        pad_ref[i, BLK:, :] = kv_ref[:, 128 * i : 128 * (i + 1)].astype(F32)


def every_stride(pad_ref, p, nb):
    tiles = [pad_ref[i, pl.ds(p, nb, stride=STRIDE), :] for i in range(pad_ref.shape[0])]
    return jnp.concatenate(tiles, axis=1)


def prep_kernel(dims, kv_ref, wk_ref, wv_ref, k_ref, kt_ref, v_ref, vt_ref, pad_ref):
    groups, dk, dv, rows, reach, nb = dims
    kw = groups * dk
    index = lax.axis_index("seq")
    win = (reach + 1) * rows
    fill_padded(pad_ref, kv_ref)
    for c in range(reach + 1):
        shard = jnp.maximum(index - reach + c, 0)
        chunk = kv_ref[pl.ds(pl.multiple_of(shard * rows, rows), rows), :]
        for g in range(groups):
            k_ref[g, c * rows : (c + 1) * rows, :] = chunk[:, g * dk : (g + 1) * dk]
            v_ref[g, c * rows : (c + 1) * rows, :] = chunk[:, kw + g * dv : kw + (g + 1) * dv]
    ck = jnp.zeros((groups * nb, dk), F32)
    cv = jnp.zeros((groups * nb, dv), F32)
    for p in range(BLK):
        at = every_stride(pad_ref, p, nb).astype(BF16)
        ck += mm(stack_groups(at[:, :kw], groups, dk), wk_ref[p * dk : (p + 1) * dk, :], 1, 0)
        cv += mm(stack_groups(at[:, kw:], groups, dv), wv_ref[p * dv : (p + 1) * dv, :], 1, 0)
    for g in range(groups):
        k_ref[g, win:, :] = ck[g * nb : (g + 1) * nb].astype(BF16)
        v_ref[g, win:, :] = cv[g * nb : (g + 1) * nb].astype(BF16)
        kt_ref[g] = k_ref[g].T
        vt_ref[g] = v_ref[g].T


def prep(kv_all, wk, wv, groups, rows, reach):
    dk, dv = wk.shape[1], wv.shape[1]
    nb = kv_all.shape[0] // STRIDE
    total = (reach + 1) * rows + nb
    dims = (groups, dk, dv, rows, reach, nb)
    sds = lambda *s: jax.ShapeDtypeStruct(s, BF16)
    return pl.pallas_call(
        functools.partial(prep_kernel, dims),
        out_shape=(
            sds(groups, total, dk),
            sds(groups, dk, total),
            sds(groups, total, dv),
            sds(groups, dv, total),
        ),
        in_specs=[full()] * 3,
        out_specs=(full(),) * 4,
        scratch_shapes=[pltpu.VMEM((kv_all.shape[1] // 128, kv_all.shape[0] + BLK, 128), F32)],
        compiler_params=pltpu.CompilerParams(vmem_limit_bytes=VLIM),
    )(kv_all, wk, wv)


def back_kernel(dims, gc_ref, kv_ref, wk_ref, wv_ref, gwk_ref, gwv_ref, own_ref, pad_ref, gf_ref, own_s):
    groups, dk, dv, rows, nb, off = dims
    kw = groups * dk
    index = lax.axis_index("seq")
    per = gwk_ref.shape[0] // dk
    blocks = rows // STRIDE
    fill_padded(pad_ref, kv_ref)
    gk = gc_ref[:, :dk]
    gv = gc_ref[:, off : off + dv]
    for i in range(per):
        at = every_stride(pad_ref, index * per + i, nb)
        kst = stack_groups(at[:, :kw], groups, dk).T.astype(BF16)
        vst = stack_groups(at[:, kw:], groups, dv).T.astype(BF16)
        gwk_ref[i * dk : (i + 1) * dk, :] = mm(kst, gk, 1, 0).astype(BF16)
        gwv_ref[i * dv : (i + 1) * dv, :] = mm(vst, gv, 1, 0).astype(BF16)
    for g in range(groups):
        gf_ref[g, 0:nb, :] = gc_ref[g * nb : (g + 1) * nb, :].astype(F32)
        gf_ref[g, nb:, :] = jnp.zeros((gf_ref.shape[1] - nb, gf_ref.shape[2]), F32)
    base = pl.multiple_of(index * blocks, blocks)
    ahead = [gf_ref[g, pl.ds(base, blocks + 8), :] for g in range(groups)]
    near = jnp.concatenate([x[1 : blocks + 1] for x in ahead], axis=0)
    far = jnp.concatenate([x[2 : blocks + 2] for x in ahead], axis=0)
    near, far = near.astype(BF16), far.astype(BF16)
    for q in range(STRIDE):
        lo, hi = q, q + STRIDE
        k = mm(far[:, :dk], wk_ref[lo * dk : (lo + 1) * dk, :], 1, 1)
        k += mm(near[:, :dk], wk_ref[hi * dk : (hi + 1) * dk, :], 1, 1)
        v = mm(far[:, off : off + dv], wv_ref[lo * dv : (lo + 1) * dv, :], 1, 1)
        v += mm(near[:, off : off + dv], wv_ref[hi * dv : (hi + 1) * dv, :], 1, 1)
        parts = [k[g * blocks : (g + 1) * blocks] for g in range(groups)]
        parts += [v[g * blocks : (g + 1) * blocks] for g in range(groups)]
        row = jnp.concatenate(parts, axis=1)
        for i in range(own_s.shape[0]):
            own_s[i, pl.ds(q, blocks, stride=STRIDE), :] = row[:, 128 * i : 128 * (i + 1)]
    for i in range(own_s.shape[0]):
        own_ref[:, 128 * i : 128 * (i + 1)] = own_s[i]


def back(gc, kv_all, wk, wv, groups, rows, off, devices):
    dk, dv = wk.shape[1], wv.shape[1]
    nb = kv_all.shape[0] // STRIDE
    dims = (groups, dk, dv, rows, nb, off)
    return pl.pallas_call(
        functools.partial(back_kernel, dims),
        out_shape=(
            jax.ShapeDtypeStruct((wk.shape[0] // devices, dk), BF16),
            jax.ShapeDtypeStruct((wv.shape[0] // devices, dv), BF16),
            jax.ShapeDtypeStruct((rows, kv_all.shape[1]), F32),
        ),
        in_specs=[full()] * 4,
        out_specs=(full(),) * 3,
        scratch_shapes=[
            pltpu.VMEM((kv_all.shape[1] // 128, kv_all.shape[0] + BLK, 128), F32),
            pltpu.VMEM((groups, nb + 8, gc.shape[1]), F32),
            pltpu.VMEM((kv_all.shape[1] // 128, rows, 128), F32),
        ],
        compiler_params=pltpu.CompilerParams(vmem_limit_bytes=VLIM),
    )(gc, kv_all, wk, wv)


def sum_kernel(n, x_ref, out_ref, parts, red, gath, send1, recv1, send2, recv2):
    me = lax.axis_index("seq")
    peers = [lax.rem(me + d, n) for d in range(n)]
    barrier = pltpu.get_barrier_semaphore()
    for d in range(1, n):
        pl.semaphore_signal(barrier, inc=1, device_id={"seq": peers[d]}, device_id_type=pl.DeviceIdType.MESH)
    pl.semaphore_wait(barrier, n - 1)

    def put(src, dst, send, recv, d):
        copy = pltpu.make_async_remote_copy(
            src_ref=src,
            dst_ref=dst,
            send_sem=send.at[d],
            recv_sem=recv.at[d],
            device_id={"seq": peers[d]},
            device_id_type=pl.DeviceIdType.MESH,
        )
        copy.start()
        return copy

    out = [put(x_ref.at[peers[d]], parts.at[d], send1, recv1, d) for d in range(1, n)]
    total = x_ref[me].astype(F32)
    for d in range(1, n):
        out[d - 1].wait()
        total = total + parts[d].astype(F32)
    red[...] = total.astype(BF16)
    out = [put(red, gath.at[me], send2, recv2, d) for d in range(1, n)]
    gath[me] = red[...]
    for copy in out:
        copy.wait()
    out_ref[...] = gath[...]


def sum_seq(x):
    n = lax.axis_size("seq")
    shape = (n, x.shape[0] // n, x.shape[1])
    out = pl.pallas_call(
        functools.partial(sum_kernel, n),
        out_shape=jax.ShapeDtypeStruct(shape, BF16),
        in_specs=[full()],
        out_specs=full(),
        scratch_shapes=[
            pltpu.VMEM(shape, BF16),
            pltpu.VMEM(shape[1:], BF16),
            pltpu.VMEM(shape, BF16),
            *[pltpu.SemaphoreType.DMA((n,))] * 4,
        ],
        compiler_params=pltpu.CompilerParams(collective_id=0, has_side_effects=True, vmem_limit_bytes=VLIM),
    )(x.reshape(shape))
    return out.reshape(x.shape)


def bias_win(index, rows, reach):
    count = (reach + 1) * rows
    j = lax.broadcasted_iota(jnp.int32, (count, 2 * rows), 0) - reach * rows
    t = lax.broadcasted_iota(jnp.int32, (count, 2 * rows), 1)
    t = jnp.where(t >= rows, t - rows, t)
    ok = (j <= t) & (t - j < WIN) & (j + index * rows >= 0)
    return jnp.where(ok, 0.0, NEG).astype(F32)


def bias_cmp(index, rows, nb):
    b = lax.broadcasted_iota(jnp.int32, (nb, 2 * rows), 0)
    t = lax.broadcasted_iota(jnp.int32, (nb, 2 * rows), 1)
    t = jnp.where(t >= rows, t - rows, t)
    return jnp.where(STRIDE * b <= t + index * rows + 1, 0.0, NEG).astype(F32)


def branch(s, cp, bias, gate, scaling):
    s = s * (scaling * math.log2(math.e)) + bias
    e = jnp.exp2(s - jnp.max(s, axis=0, keepdims=True))
    inv = 1.0 / jnp.sum(e, axis=0, keepdims=True)
    gg = jnp.sum(e * cp, axis=0, keepdims=True) * inv
    w = (e * (gate * inv)).astype(BF16)
    gs = (e * (cp - gg) * (gate * (inv * scaling))).astype(BF16)
    return gg, w, gs


def load_pair(i, rows, dk, dv, q_ref, c_ref, qs, cs):
    base = 2 * i * rows
    both = q_ref[:, 2 * i * dk : 2 * (i + 1) * dk]
    qs[base : base + rows, :] = both[:, :dk]
    qs[base + rows : base + 2 * rows, :] = both[:, dk:]
    cs[base : base + rows, :] = c_ref[:, 2 * i * dv : (2 * i + 1) * dv]
    cs[base + rows : base + 2 * rows, :] = c_ref[:, (2 * i + 1) * dv : (2 * i + 2) * dv]
    return qs[base : base + 2 * rows, :], cs[base : base + 2 * rows, :]


def pair_gate(gate_t, first, i):
    return jnp.concatenate([gate_t[2 * i : 2 * i + 1, :], gate_t[2 * i + 1 : 2 * i + 2, :]], axis=1)


def cmp_kernel(dims, q_ref, c_ref, k_ref, v_ref, gate_ref, out_ref, bias, gate_s, qs, cs, ws, gss):
    rows, per, dk, dv, nb, off, reach = dims
    win = (reach + 1) * rows
    step = pl.program_id(0)

    @pl.when(step == 0)
    def _():
        bias[...] = bias_cmp(lax.axis_index("seq"), rows, nb)
        gate_s[...] = gate_ref[...].T

    gate_t = gate_s[pl.ds(pl.multiple_of(step * per, per), per), :]
    k = k_ref[0, win:, :]
    v = v_ref[0, win:, :]
    scaling = 1.0 / math.sqrt(dk)
    for i in range(per // 2):
        q2, c2 = load_pair(i, rows, dk, dv, q_ref, c_ref, qs, cs)
        gate = pair_gate(gate_t, 0, i)
        _, w, gs = branch(mm(k, q2, 1, 1), mm(v, c2, 1, 1), bias[...], gate, scaling)
        ws[:, 2 * i * rows : 2 * (i + 1) * rows] = w
        gss[:, 2 * i * rows : 2 * (i + 1) * rows] = gs
    out_ref[:, :dk] = mm(gss[...], qs[...], 1, 0).astype(BF16)
    if off > dk:
        out_ref[:, dk:off] = jnp.zeros((nb, off - dk), BF16)
    out_ref[:, off:] = mm(ws[...], cs[...], 1, 0).astype(BF16)


def cmp_grads(q, c, kall, vall, gate, groups, reach, nb, off):
    rows = q.shape[0]
    heads = gate.shape[1]
    per = heads // groups
    dk, dv, total = kall.shape[2], vall.shape[2], kall.shape[1]
    dims = (rows, per, dk, dv, nb, off, reach)
    return pl.pallas_call(
        functools.partial(cmp_kernel, dims),
        grid=(groups,),
        out_shape=jax.ShapeDtypeStruct((groups * nb, off + dv), BF16),
        in_specs=[
            pl.BlockSpec((rows, per * dk), lambda g: (0, g)),
            pl.BlockSpec((rows, per * dv), lambda g: (0, g)),
            pl.BlockSpec((1, total, dk), lambda g: (g, 0, 0)),
            pl.BlockSpec((1, total, dv), lambda g: (g, 0, 0)),
            pl.BlockSpec((rows, heads), lambda g: (0, 0)),
        ],
        out_specs=pl.BlockSpec((nb, off + dv), lambda g: (g, 0)),
        scratch_shapes=[
            pltpu.VMEM((nb, 2 * rows), F32),
            pltpu.VMEM((heads, rows), F32),
            pltpu.VMEM((per * rows, dk), BF16),
            pltpu.VMEM((per * rows, dv), BF16),
            pltpu.VMEM((nb, per * rows), BF16),
            pltpu.VMEM((nb, per * rows), BF16),
        ],
        compiler_params=pltpu.CompilerParams(vmem_limit_bytes=VLIM),
    )(q, c, kall, vall, gate)


def main_kernel(dims, alias, *refs):
    rows, hc, chunks, dk, dv, nb, off, reach, first = dims
    q_ref, c_ref, k_ref, kt_ref, v_ref, vt_ref, gc_ref, gw_ref = refs[:8]
    refs = refs[10:] if alias else refs[8:]
    att_ref, gq_ref, send_ref, own_ref, ggc_ref, ggw_ref = refs[:6]
    bias, gct, gwt, ggct, ggwt, qs, cs, ws, gss, acck, accv = refs[6:]
    win = (reach + 1) * rows
    lead = reach * rows
    g, part = pl.program_id(0), pl.program_id(1)
    step = g * chunks + part

    @pl.when(step == 0)
    def _():
        index = lax.axis_index("seq")
        bias[:win, :] = bias_win(index, rows, reach)
        bias[win:, :] = bias_cmp(index, rows, nb)
        gct[...] = gc_ref[...].T
        gwt[...] = gw_ref[...].T

    row0 = pl.multiple_of(step * hc, hc)
    head0 = pl.multiple_of(first * hc * chunks + step * hc, hc)
    gate_c = gct[pl.ds(head0, hc), :]
    gate_w = gwt[pl.ds(head0, hc), :]
    scaling = 1.0 / math.sqrt(dk)
    rows_c, rows_w = [], []
    for i in range(hc // 2):
        q2, c2 = load_pair(i, rows, dk, dv, q_ref, c_ref, qs, cs)
        s = mm(k_ref[0], q2, 1, 1)
        cp = mm(v_ref[0], c2, 1, 1)
        gg_w, w_w, gs_w = branch(s[:win], cp[:win], bias[:win, :], pair_gate(gate_w, 0, i), scaling)
        gg_c, w_c, gs_c = branch(s[win:], cp[win:], bias[win:, :], pair_gate(gate_c, 0, i), scaling)
        cols = slice(2 * i * rows, 2 * (i + 1) * rows)
        ws[:win, cols] = w_w
        ws[win:, cols] = w_c
        gss[:win, cols] = gs_w
        gss[win:, cols] = gs_c
        rows_w += [gg_w[:, :rows], gg_w[:, rows:]]
        rows_c += [gg_c[:, :rows], gg_c[:, rows:]]
        att = mm(vt_ref[0], ws[:, cols], 1, 0)
        gq = mm(kt_ref[0], gss[:, cols], 1, 0)
        att = jnp.concatenate([att[:, :rows], att[:, rows:]], axis=0)
        gq = jnp.concatenate([gq[:, :rows], gq[:, rows:]], axis=0)
        att_ref[:, 2 * i * dv : 2 * (i + 1) * dv] = att.T.astype(BF16)
        gq_ref[:, 2 * i * dk : 2 * (i + 1) * dk] = gq.T.astype(BF16)
    ggct[pl.ds(row0, hc), :] = jnp.concatenate(rows_c, axis=0)
    ggwt[pl.ds(row0, hc), :] = jnp.concatenate(rows_w, axis=0)
    gk = mm(gss[:win, :], qs[...], 1, 0)
    gv = mm(ws[:win, :], cs[...], 1, 0)

    @pl.when(part == 0)
    def _():
        acck[...] = gk
        accv[...] = gv

    @pl.when(part > 0)
    def _():
        acck[...] += gk
        accv[...] += gv

    @pl.when(part == chunks - 1)
    def _():
        send_ref[0, :, :dk] = acck[:lead, :].astype(BF16)
        send_ref[0, :, off:] = accv[:lead, :].astype(BF16)
        own_ref[0, :, :dk] = acck[lead:, :]
        own_ref[0, :, off:] = accv[lead:, :]
        if off > dk:
            send_ref[0, :, dk:off] = jnp.zeros((lead, off - dk), BF16)
            own_ref[0, :, dk:off] = jnp.zeros((rows, off - dk), F32)
        ggc_ref[...] = ggct[...].T
        ggw_ref[...] = ggwt[...].T


def attend(q, c, prepped, gate_c, gate_w, first, count, groups, reach, nb, off, into):
    kall, kt, vall, vt = prepped
    rows = q.shape[0]
    heads = gate_c.shape[1]
    per = heads // groups
    hc = 8
    chunks = per // hc
    dk, dv, total = kall.shape[2], vall.shape[2], kall.shape[1]
    win = (reach + 1) * rows
    dims = (rows, hc, chunks, dk, dv, nb, off, reach, first)
    col = lambda g, p: (0, (first + g) * chunks + p)
    grp = lambda g, p: (first + g, 0, 0)
    whole = lambda g, p: (0, 0)
    sds = jax.ShapeDtypeStruct
    in_specs = [
        pl.BlockSpec((rows, hc * dk), col),
        pl.BlockSpec((rows, hc * dv), col),
        pl.BlockSpec((1, total, dk), grp),
        pl.BlockSpec((1, dk, total), grp),
        pl.BlockSpec((1, total, dv), grp),
        pl.BlockSpec((1, dv, total), grp),
        pl.BlockSpec((rows, heads), whole),
        pl.BlockSpec((rows, heads), whole),
    ]
    args = [q, c, kall, kt, vall, vt, gate_c, gate_w]
    aliases = {}
    if into is not None:
        in_specs += [pl.BlockSpec(memory_space=pl.ANY)] * 2
        args += list(into)
        aliases = {8: 0, 9: 1}
    flops = 2 * 2 * 3 * rows * per * count * total * (dk + dv)
    return pl.pallas_call(
        functools.partial(main_kernel, dims, into is not None),
        grid=(count, chunks),
        out_shape=(
            sds((rows, heads * dv), BF16),
            sds((rows, heads * dk), BF16),
            sds((count, reach * rows, off + dv), BF16),
            sds((count, rows, off + dv), F32),
            sds((rows, per * count), F32),
            sds((rows, per * count), F32),
        ),
        in_specs=in_specs,
        out_specs=(
            pl.BlockSpec((rows, hc * dv), col),
            pl.BlockSpec((rows, hc * dk), col),
            pl.BlockSpec((1, reach * rows, off + dv), lambda g, p: (g, 0, 0)),
            pl.BlockSpec((1, rows, off + dv), lambda g, p: (g, 0, 0)),
            pl.BlockSpec((rows, per * count), whole),
            pl.BlockSpec((rows, per * count), whole),
        ),
        scratch_shapes=[
            pltpu.VMEM((total, 2 * rows), F32),
            pltpu.VMEM((heads, rows), F32),
            pltpu.VMEM((heads, rows), F32),
            pltpu.VMEM((per * count, rows), F32),
            pltpu.VMEM((per * count, rows), F32),
            pltpu.VMEM((hc * rows, dk), BF16),
            pltpu.VMEM((hc * rows, dv), BF16),
            pltpu.VMEM((total, hc * rows), BF16),
            pltpu.VMEM((total, hc * rows), BF16),
            pltpu.VMEM((win, dk), F32),
            pltpu.VMEM((win, dv), F32),
        ],
        input_output_aliases=aliases,
        cost_estimate=pl.CostEstimate(flops=4 * flops, bytes_accessed=rows * heads * (dk + dv) * 4, transcendentals=0),
        compiler_params=pltpu.CompilerParams(vmem_limit_bytes=VLIM),
    )(*args)


def finish_kernel(dims, cmp_ref, *refs):
    groups, dk, dv, off, halves = dims
    k_ref, v_ref = refs[-2:]
    ins = refs[:-2]
    kw = groups * dk
    each = groups // halves
    per_half = len(ins) // halves
    ks, vs = [], []
    for half in range(halves):
        mine = ins[half * per_half : (half + 1) * per_half]
        for g in range(each):
            total = mine[0][g]
            for ref in mine[1:]:
                total = total + ref[g].astype(F32)
            ks.append(total[:, :dk])
            vs.append(total[:, off:])
    k_ref[...] = (jnp.concatenate(ks, axis=1) + cmp_ref[:, :kw]).astype(BF16)
    v_ref[...] = (jnp.concatenate(vs, axis=1) + cmp_ref[:, kw:]).astype(BF16)


def finish(own_cmp, parts, groups, dk, dv, off, halves):
    rows = own_cmp.shape[0]
    return pl.pallas_call(
        functools.partial(finish_kernel, (groups, dk, dv, off, halves)),
        out_shape=(
            jax.ShapeDtypeStruct((rows, groups * dk), BF16),
            jax.ShapeDtypeStruct((rows, groups * dv), BF16),
        ),
        in_specs=[full()] * (1 + len(parts)),
        out_specs=(full(),) * 2,
        compiler_params=pltpu.CompilerParams(vmem_limit_bytes=VLIM),
    )(own_cmp, *parts)


def send_back(send, rows, reach):
    devices = lax.axis_size("seq")
    got = []
    for distance in range(1, reach + 1):
        at = (reach - distance) * rows
        pairs = [(i, i - distance) for i in range(devices) if i - distance >= 0]
        got.append(lax.ppermute(send[:, at : at + rows], "seq", pairs))
    return got


def on_device(queries, keys_in, values_in, gate_cmp, gate_win, cotangent, compress_key, compress_value):
    rows = queries.shape[1]
    dk, dv = compress_key.shape[1], compress_value.shape[1]
    groups = keys_in.shape[2] // dk
    devices = lax.axis_size("seq")
    reach = (WIN + rows - 1) // rows
    off = up128(dk)
    q, c = queries[0], cotangent[0]
    gc, gw = gate_cmp[0], gate_win[0]
    kv = jnp.concatenate([keys_in[0], values_in[0]], axis=1)
    kv_all = lax.all_gather(kv, "seq", axis=0, tiled=True)
    nb = kv_all.shape[0] // STRIDE
    prepped = prep(kv_all, compress_key, compress_value, groups, rows, reach)
    part = cmp_grads(q, c, prepped[0], prepped[2], gc, groups, reach, nb, off)
    total = sum_seq(part)
    gwk, gwv, own_cmp = back(total, kv_all, compress_key, compress_value, groups, rows, off, devices)
    kall, gwk, gwv = lax.optimization_barrier((prepped[0], gwk, gwv))
    gwk_sum, gwv_sum = lax.psum(gwk, "dp"), lax.psum(gwv, "dp")
    prepped = (kall, *prepped[1:])
    att, gq, send, own, ggc, ggw = attend(
        q, c, prepped, gc, gw, 0, groups, groups, reach, nb, off, None
    )
    send, gwk_sum, gwv_sum = lax.optimization_barrier((send, gwk_sum, gwv_sum))
    got = send_back(send, rows, reach)
    gk, gv = finish(own_cmp, [own, *got], groups, dk, dv, off, 1)
    return (
        att[None],
        gq[None],
        gk[None],
        gv[None],
        ggc[None],
        ggw[None],
        gwk_sum.astype(F32),
        gwv_sum.astype(F32),
    )


def solution(mesh):
    tokens = P("dp", "seq", None)
    in_specs = (tokens,) * 6 + (P(), P())
    out_specs = (tokens,) * 6 + (P("seq", None), P("seq", None))
    return jax.shard_map(on_device, mesh=mesh, in_specs=in_specs, out_specs=out_specs, check_vma=False)
```

```python
import functools
import math

import jax
import jax.numpy as jnp
from jax import lax
from jax.experimental import pallas as pl
from jax.experimental.pallas import tpu as pltpu
from jax.sharding import PartitionSpec as P

BLK = 32
STRIDE = 16
WIN = 512
NEG = -1e30
F32 = jnp.float32
BF16 = jnp.bfloat16
VLIM = 56 * 1024 * 1024


def mm(a, b, ca, cb):
    return lax.dot_general(a, b, (((ca,), (cb,)), ((), ())), preferred_element_type=F32)


def full(memory=pltpu.VMEM):
    return pl.BlockSpec(memory_space=memory)


def up128(n):
    return (n + 127) // 128 * 128


def stack_groups(rows, groups, width):
    return jnp.concatenate([rows[:, g * width : (g + 1) * width] for g in range(groups)], axis=0)


def fill_padded(pad_ref, kv_ref):
    for i in range(pad_ref.shape[0]):
        pad_ref[i, 0:BLK, :] = jnp.zeros((BLK, 128), F32)
        pad_ref[i, BLK:, :] = kv_ref[:, 128 * i : 128 * (i + 1)].astype(F32)


def every_stride(pad_ref, p, nb):
    tiles = [pad_ref[i, pl.ds(p, nb, stride=STRIDE), :] for i in range(pad_ref.shape[0])]
    return jnp.concatenate(tiles, axis=1)


def prep_kernel(dims, kv_ref, wk_ref, wv_ref, k_ref, kt_ref, v_ref, vt_ref, pad_ref):
    groups, dk, dv, rows, reach, nb = dims
    kw = groups * dk
    index = lax.axis_index("seq")
    win = (reach + 1) * rows
    fill_padded(pad_ref, kv_ref)
    for c in range(reach + 1):
        shard = jnp.maximum(index - reach + c, 0)
        chunk = kv_ref[pl.ds(pl.multiple_of(shard * rows, rows), rows), :]
        for g in range(groups):
            k_ref[g, c * rows : (c + 1) * rows, :] = chunk[:, g * dk : (g + 1) * dk]
            v_ref[g, c * rows : (c + 1) * rows, :] = chunk[:, kw + g * dv : kw + (g + 1) * dv]
    ck = jnp.zeros((groups * nb, dk), F32)
    cv = jnp.zeros((groups * nb, dv), F32)
    for p in range(BLK):
        at = every_stride(pad_ref, p, nb).astype(BF16)
        ck += mm(stack_groups(at[:, :kw], groups, dk), wk_ref[p * dk : (p + 1) * dk, :], 1, 0)
        cv += mm(stack_groups(at[:, kw:], groups, dv), wv_ref[p * dv : (p + 1) * dv, :], 1, 0)
    for g in range(groups):
        k_ref[g, win:, :] = ck[g * nb : (g + 1) * nb].astype(BF16)
        v_ref[g, win:, :] = cv[g * nb : (g + 1) * nb].astype(BF16)
        kt_ref[g] = k_ref[g].T
        vt_ref[g] = v_ref[g].T


def prep(kv_all, wk, wv, groups, rows, reach):
    dk, dv = wk.shape[1], wv.shape[1]
    nb = kv_all.shape[0] // STRIDE
    total = (reach + 1) * rows + nb
    dims = (groups, dk, dv, rows, reach, nb)
    sds = lambda *s: jax.ShapeDtypeStruct(s, BF16)
    return pl.pallas_call(
        functools.partial(prep_kernel, dims),
        out_shape=(
            sds(groups, total, dk),
            sds(groups, dk, total),
            sds(groups, total, dv),
            sds(groups, dv, total),
        ),
        in_specs=[full()] * 3,
        out_specs=(full(),) * 4,
        scratch_shapes=[pltpu.VMEM((kv_all.shape[1] // 128, kv_all.shape[0] + BLK, 128), F32)],
        compiler_params=pltpu.CompilerParams(vmem_limit_bytes=VLIM),
    )(kv_all, wk, wv)


def back_kernel(dims, gc_ref, kv_ref, wk_ref, wv_ref, gwk_ref, gwv_ref, own_ref, pad_ref, gf_ref, own_s):
    groups, dk, dv, rows, nb, off = dims
    kw = groups * dk
    index = lax.axis_index("seq")
    per = gwk_ref.shape[0] // dk
    blocks = rows // STRIDE
    fill_padded(pad_ref, kv_ref)
    gk = gc_ref[:, :dk]
    gv = gc_ref[:, off : off + dv]
    for i in range(per):
        at = every_stride(pad_ref, index * per + i, nb)
        kst = stack_groups(at[:, :kw], groups, dk).T.astype(BF16)
        vst = stack_groups(at[:, kw:], groups, dv).T.astype(BF16)
        gwk_ref[i * dk : (i + 1) * dk, :] = mm(kst, gk, 1, 0).astype(BF16)
        gwv_ref[i * dv : (i + 1) * dv, :] = mm(vst, gv, 1, 0).astype(BF16)
    for g in range(groups):
        gf_ref[g, 0:nb, :] = gc_ref[g * nb : (g + 1) * nb, :].astype(F32)
        gf_ref[g, nb:, :] = jnp.zeros((gf_ref.shape[1] - nb, gf_ref.shape[2]), F32)
    base = pl.multiple_of(index * blocks, blocks)
    ahead = [gf_ref[g, pl.ds(base, blocks + 8), :] for g in range(groups)]
    near = jnp.concatenate([x[1 : blocks + 1] for x in ahead], axis=0)
    far = jnp.concatenate([x[2 : blocks + 2] for x in ahead], axis=0)
    near, far = near.astype(BF16), far.astype(BF16)
    for q in range(STRIDE):
        lo, hi = q, q + STRIDE
        k = mm(far[:, :dk], wk_ref[lo * dk : (lo + 1) * dk, :], 1, 1)
        k += mm(near[:, :dk], wk_ref[hi * dk : (hi + 1) * dk, :], 1, 1)
        v = mm(far[:, off : off + dv], wv_ref[lo * dv : (lo + 1) * dv, :], 1, 1)
        v += mm(near[:, off : off + dv], wv_ref[hi * dv : (hi + 1) * dv, :], 1, 1)
        parts = [k[g * blocks : (g + 1) * blocks] for g in range(groups)]
        parts += [v[g * blocks : (g + 1) * blocks] for g in range(groups)]
        row = jnp.concatenate(parts, axis=1)
        for i in range(own_s.shape[0]):
            own_s[i, pl.ds(q, blocks, stride=STRIDE), :] = row[:, 128 * i : 128 * (i + 1)]
    for i in range(own_s.shape[0]):
        own_ref[:, 128 * i : 128 * (i + 1)] = own_s[i]


def back(gc, kv_all, wk, wv, groups, rows, off, devices):
    dk, dv = wk.shape[1], wv.shape[1]
    nb = kv_all.shape[0] // STRIDE
    dims = (groups, dk, dv, rows, nb, off)
    return pl.pallas_call(
        functools.partial(back_kernel, dims),
        out_shape=(
            jax.ShapeDtypeStruct((wk.shape[0] // devices, dk), BF16),
            jax.ShapeDtypeStruct((wv.shape[0] // devices, dv), BF16),
            jax.ShapeDtypeStruct((rows, kv_all.shape[1]), F32),
        ),
        in_specs=[full()] * 4,
        out_specs=(full(),) * 3,
        scratch_shapes=[
            pltpu.VMEM((kv_all.shape[1] // 128, kv_all.shape[0] + BLK, 128), F32),
            pltpu.VMEM((groups, nb + 8, gc.shape[1]), F32),
            pltpu.VMEM((kv_all.shape[1] // 128, rows, 128), F32),
        ],
        compiler_params=pltpu.CompilerParams(vmem_limit_bytes=VLIM),
    )(gc, kv_all, wk, wv)


def sum_kernel(n, x_ref, out_ref, parts, red, gath, send1, recv1, send2, recv2):
    me = lax.axis_index("seq")
    peers = [lax.rem(me + d, n) for d in range(n)]
    barrier = pltpu.get_barrier_semaphore()
    for d in range(1, n):
        pl.semaphore_signal(barrier, inc=1, device_id={"seq": peers[d]}, device_id_type=pl.DeviceIdType.MESH)
    pl.semaphore_wait(barrier, n - 1)

    def put(src, dst, send, recv, d):
        copy = pltpu.make_async_remote_copy(
            src_ref=src,
            dst_ref=dst,
            send_sem=send.at[d],
            recv_sem=recv.at[d],
            device_id={"seq": peers[d]},
            device_id_type=pl.DeviceIdType.MESH,
        )
        copy.start()
        return copy

    out = [put(x_ref.at[peers[d]], parts.at[d], send1, recv1, d) for d in range(1, n)]
    total = x_ref[me].astype(F32)
    for d in range(1, n):
        out[d - 1].wait()
        total = total + parts[d].astype(F32)
    red[...] = total.astype(BF16)
    out = [put(red, gath.at[me], send2, recv2, d) for d in range(1, n)]
    gath[me] = red[...]
    for copy in out:
        copy.wait()
    out_ref[...] = gath[...]


def sum_seq(x):
    n = lax.axis_size("seq")
    shape = (n, x.shape[0] // n, x.shape[1])
    out = pl.pallas_call(
        functools.partial(sum_kernel, n),
        out_shape=jax.ShapeDtypeStruct(shape, BF16),
        in_specs=[full()],
        out_specs=full(),
        scratch_shapes=[
            pltpu.VMEM(shape, BF16),
            pltpu.VMEM(shape[1:], BF16),
            pltpu.VMEM(shape, BF16),
            *[pltpu.SemaphoreType.DMA((n,))] * 4,
        ],
        compiler_params=pltpu.CompilerParams(collective_id=0, has_side_effects=True, vmem_limit_bytes=VLIM),
    )(x.reshape(shape))
    return out.reshape(x.shape)


def gather_kernel(n, k_ref, v_ref, out_ref, gath, own, send1, recv1, send2, recv2):
    me = lax.axis_index("seq")
    sibling = me + 1 - 2 * lax.rem(me, 2)
    pairs = n // 2
    kw = k_ref.shape[1]
    peers = [lax.rem(me + 2 * d, n) for d in range(1, pairs)]
    origins = [lax.rem(me + n - 2 * d, n) for d in range(1, pairs)]
    barrier = pltpu.get_barrier_semaphore()
    for peer in [sibling, *peers]:
        pl.semaphore_signal(barrier, inc=1, device_id={"seq": peer}, device_id_type=pl.DeviceIdType.MESH)
    own[:, :kw] = k_ref[...]
    own[:, kw:] = v_ref[...]
    pl.semaphore_wait(barrier, pairs)

    def put(src, slot, send, recv, d, peer):
        copy = pltpu.make_async_remote_copy(
            src_ref=src,
            dst_ref=gath.at[slot],
            send_sem=send.at[d],
            recv_sem=recv.at[d],
            device_id={"seq": peer},
            device_id_type=pl.DeviceIdType.MESH,
        )
        copy.start()
        return copy

    first = [put(own, me, send1, recv1, d, peers[d - 1]) for d in range(1, pairs)]
    second = [put(own, me, send2, recv2, 0, sibling)]
    gath[me] = own[...]
    for d in range(1, pairs):
        first[d - 1].wait()
        second.append(put(gath.at[origins[d - 1]], origins[d - 1], send2, recv2, d, sibling))
    for copy in second:
        copy.wait()
    out_ref[...] = gath[...]


def gather_seq(k, v):
    n = lax.axis_size("seq")
    width = k.shape[1] + v.shape[1]
    shape = (n, k.shape[0], width)
    out = pl.pallas_call(
        functools.partial(gather_kernel, n),
        out_shape=jax.ShapeDtypeStruct(shape, BF16),
        in_specs=[full()] * 2,
        out_specs=full(),
        scratch_shapes=[
            pltpu.VMEM(shape, BF16),
            pltpu.VMEM(shape[1:], BF16),
            *[pltpu.SemaphoreType.DMA((n // 2,))] * 4,
        ],
        compiler_params=pltpu.CompilerParams(collective_id=1, has_side_effects=True, vmem_limit_bytes=VLIM),
    )(k, v)
    return out.reshape(n * k.shape[0], width)


def bias_win(index, rows, reach):
    count = (reach + 1) * rows
    j = lax.broadcasted_iota(jnp.int32, (count, 2 * rows), 0) - reach * rows
    t = lax.broadcasted_iota(jnp.int32, (count, 2 * rows), 1)
    t = jnp.where(t >= rows, t - rows, t)
    ok = (j <= t) & (t - j < WIN) & (j + index * rows >= 0)
    return jnp.where(ok, 0.0, NEG).astype(F32)


def bias_cmp(index, rows, nb):
    b = lax.broadcasted_iota(jnp.int32, (nb, 2 * rows), 0)
    t = lax.broadcasted_iota(jnp.int32, (nb, 2 * rows), 1)
    t = jnp.where(t >= rows, t - rows, t)
    return jnp.where(STRIDE * b <= t + index * rows + 1, 0.0, NEG).astype(F32)


def branch(s, cp, bias, gate, scaling):
    s = s * (scaling * math.log2(math.e)) + bias
    e = jnp.exp2(s - jnp.max(s, axis=0, keepdims=True))
    inv = 1.0 / jnp.sum(e, axis=0, keepdims=True)
    gg = jnp.sum(e * cp, axis=0, keepdims=True) * inv
    w = (e * (gate * inv)).astype(BF16)
    gs = (e * (cp - gg) * (gate * (inv * scaling))).astype(BF16)
    return gg, w, gs


def load_pair(i, rows, dk, dv, q_ref, c_ref, qs, cs):
    base = 2 * i * rows
    both = q_ref[:, 2 * i * dk : 2 * (i + 1) * dk]
    qs[base : base + rows, :] = both[:, :dk]
    qs[base + rows : base + 2 * rows, :] = both[:, dk:]
    cs[base : base + rows, :] = c_ref[:, 2 * i * dv : (2 * i + 1) * dv]
    cs[base + rows : base + 2 * rows, :] = c_ref[:, (2 * i + 1) * dv : (2 * i + 2) * dv]
    return qs[base : base + 2 * rows, :], cs[base : base + 2 * rows, :]


def pair_gate(gate_t, first, i):
    return jnp.concatenate([gate_t[2 * i : 2 * i + 1, :], gate_t[2 * i + 1 : 2 * i + 2, :]], axis=1)


def cmp_kernel(dims, q_ref, c_ref, k_ref, v_ref, gate_ref, out_ref, bias, gate_s, qs, cs, ws, gss):
    rows, per, dk, dv, nb, off, reach = dims
    win = (reach + 1) * rows
    step = pl.program_id(0)

    @pl.when(step == 0)
    def _():
        bias[...] = bias_cmp(lax.axis_index("seq"), rows, nb)
        gate_s[...] = gate_ref[...].T

    gate_t = gate_s[pl.ds(pl.multiple_of(step * per, per), per), :]
    k = k_ref[0, win:, :]
    v = v_ref[0, win:, :]
    scaling = 1.0 / math.sqrt(dk)
    for i in range(per // 2):
        q2, c2 = load_pair(i, rows, dk, dv, q_ref, c_ref, qs, cs)
        gate = pair_gate(gate_t, 0, i)
        _, w, gs = branch(mm(k, q2, 1, 1), mm(v, c2, 1, 1), bias[...], gate, scaling)
        ws[:, 2 * i * rows : 2 * (i + 1) * rows] = w
        gss[:, 2 * i * rows : 2 * (i + 1) * rows] = gs
    out_ref[:, :dk] = mm(gss[...], qs[...], 1, 0).astype(BF16)
    if off > dk:
        out_ref[:, dk:off] = jnp.zeros((nb, off - dk), BF16)
    out_ref[:, off:] = mm(ws[...], cs[...], 1, 0).astype(BF16)


def cmp_grads(q, c, kall, vall, gate, groups, reach, nb, off):
    rows = q.shape[0]
    heads = gate.shape[1]
    per = heads // groups
    dk, dv, total = kall.shape[2], vall.shape[2], kall.shape[1]
    dims = (rows, per, dk, dv, nb, off, reach)
    return pl.pallas_call(
        functools.partial(cmp_kernel, dims),
        grid=(groups,),
        out_shape=jax.ShapeDtypeStruct((groups * nb, off + dv), BF16),
        in_specs=[
            pl.BlockSpec((rows, per * dk), lambda g: (0, g)),
            pl.BlockSpec((rows, per * dv), lambda g: (0, g)),
            pl.BlockSpec((1, total, dk), lambda g: (g, 0, 0)),
            pl.BlockSpec((1, total, dv), lambda g: (g, 0, 0)),
            pl.BlockSpec((rows, heads), lambda g: (0, 0)),
        ],
        out_specs=pl.BlockSpec((nb, off + dv), lambda g: (g, 0)),
        scratch_shapes=[
            pltpu.VMEM((nb, 2 * rows), F32),
            pltpu.VMEM((heads, rows), F32),
            pltpu.VMEM((per * rows, dk), BF16),
            pltpu.VMEM((per * rows, dv), BF16),
            pltpu.VMEM((nb, per * rows), BF16),
            pltpu.VMEM((nb, per * rows), BF16),
        ],
        compiler_params=pltpu.CompilerParams(vmem_limit_bytes=VLIM),
    )(q, c, kall, vall, gate)


def main_kernel(dims, alias, *refs):
    rows, hc, chunks, dk, dv, nb, off, reach, first = dims
    q_ref, c_ref, k_ref, kt_ref, v_ref, vt_ref, gc_ref, gw_ref = refs[:8]
    refs = refs[10:] if alias else refs[8:]
    att_ref, gq_ref, send_ref, own_ref, ggc_ref, ggw_ref = refs[:6]
    bias, gct, gwt, ggct, ggwt, qs, cs, ws, gss, acck, accv = refs[6:]
    win = (reach + 1) * rows
    lead = reach * rows
    g, part = pl.program_id(0), pl.program_id(1)
    step = g * chunks + part

    @pl.when(step == 0)
    def _():
        index = lax.axis_index("seq")
        bias[:win, :] = bias_win(index, rows, reach)
        bias[win:, :] = bias_cmp(index, rows, nb)
        gct[...] = gc_ref[...].T
        gwt[...] = gw_ref[...].T

    row0 = pl.multiple_of(step * hc, hc)
    head0 = pl.multiple_of(first * hc * chunks + step * hc, hc)
    gate_c = gct[pl.ds(head0, hc), :]
    gate_w = gwt[pl.ds(head0, hc), :]
    scaling = 1.0 / math.sqrt(dk)
    rows_c, rows_w = [], []
    for i in range(hc // 2):
        q2, c2 = load_pair(i, rows, dk, dv, q_ref, c_ref, qs, cs)
        s = mm(k_ref[0], q2, 1, 1)
        cp = mm(v_ref[0], c2, 1, 1)
        gg_w, w_w, gs_w = branch(s[:win], cp[:win], bias[:win, :], pair_gate(gate_w, 0, i), scaling)
        gg_c, w_c, gs_c = branch(s[win:], cp[win:], bias[win:, :], pair_gate(gate_c, 0, i), scaling)
        cols = slice(2 * i * rows, 2 * (i + 1) * rows)
        ws[:win, cols] = w_w
        ws[win:, cols] = w_c
        gss[:win, cols] = gs_w
        gss[win:, cols] = gs_c
        rows_w += [gg_w[:, :rows], gg_w[:, rows:]]
        rows_c += [gg_c[:, :rows], gg_c[:, rows:]]
        att = mm(vt_ref[0], ws[:, cols], 1, 0)
        gq = mm(kt_ref[0], gss[:, cols], 1, 0)
        att = jnp.concatenate([att[:, :rows], att[:, rows:]], axis=0)
        gq = jnp.concatenate([gq[:, :rows], gq[:, rows:]], axis=0)
        att_ref[:, 2 * i * dv : 2 * (i + 1) * dv] = att.T.astype(BF16)
        gq_ref[:, 2 * i * dk : 2 * (i + 1) * dk] = gq.T.astype(BF16)
    ggct[pl.ds(row0, hc), :] = jnp.concatenate(rows_c, axis=0)
    ggwt[pl.ds(row0, hc), :] = jnp.concatenate(rows_w, axis=0)
    gk = mm(gss[:win, :], qs[...], 1, 0)
    gv = mm(ws[:win, :], cs[...], 1, 0)

    @pl.when(part == 0)
    def _():
        acck[...] = gk
        accv[...] = gv

    @pl.when(part > 0)
    def _():
        acck[...] += gk
        accv[...] += gv

    @pl.when(part == chunks - 1)
    def _():
        send_ref[0, :, :dk] = acck[:lead, :].astype(BF16)
        send_ref[0, :, off:] = accv[:lead, :].astype(BF16)
        own_ref[0, :, :dk] = acck[lead:, :]
        own_ref[0, :, off:] = accv[lead:, :]
        if off > dk:
            send_ref[0, :, dk:off] = jnp.zeros((lead, off - dk), BF16)
            own_ref[0, :, dk:off] = jnp.zeros((rows, off - dk), F32)
        ggc_ref[...] = ggct[...].T
        ggw_ref[...] = ggwt[...].T


def attend(q, c, prepped, gate_c, gate_w, first, count, groups, reach, nb, off, into):
    kall, kt, vall, vt = prepped
    rows = q.shape[0]
    heads = gate_c.shape[1]
    per = heads // groups
    hc = 8
    chunks = per // hc
    dk, dv, total = kall.shape[2], vall.shape[2], kall.shape[1]
    win = (reach + 1) * rows
    dims = (rows, hc, chunks, dk, dv, nb, off, reach, first)
    col = lambda g, p: (0, (first + g) * chunks + p)
    grp = lambda g, p: (first + g, 0, 0)
    whole = lambda g, p: (0, 0)
    sds = jax.ShapeDtypeStruct
    in_specs = [
        pl.BlockSpec((rows, hc * dk), col),
        pl.BlockSpec((rows, hc * dv), col),
        pl.BlockSpec((1, total, dk), grp),
        pl.BlockSpec((1, dk, total), grp),
        pl.BlockSpec((1, total, dv), grp),
        pl.BlockSpec((1, dv, total), grp),
        pl.BlockSpec((rows, heads), whole),
        pl.BlockSpec((rows, heads), whole),
    ]
    args = [q, c, kall, kt, vall, vt, gate_c, gate_w]
    aliases = {}
    if into is not None:
        in_specs += [pl.BlockSpec(memory_space=pl.ANY)] * 2
        args += list(into)
        aliases = {8: 0, 9: 1}
    flops = 2 * 2 * 3 * rows * per * count * total * (dk + dv)
    return pl.pallas_call(
        functools.partial(main_kernel, dims, into is not None),
        grid=(count, chunks),
        out_shape=(
            sds((rows, heads * dv), BF16),
            sds((rows, heads * dk), BF16),
            sds((count, reach * rows, off + dv), BF16),
            sds((count, rows, off + dv), F32),
            sds((rows, per * count), F32),
            sds((rows, per * count), F32),
        ),
        in_specs=in_specs,
        out_specs=(
            pl.BlockSpec((rows, hc * dv), col),
            pl.BlockSpec((rows, hc * dk), col),
            pl.BlockSpec((1, reach * rows, off + dv), lambda g, p: (g, 0, 0)),
            pl.BlockSpec((1, rows, off + dv), lambda g, p: (g, 0, 0)),
            pl.BlockSpec((rows, per * count), whole),
            pl.BlockSpec((rows, per * count), whole),
        ),
        scratch_shapes=[
            pltpu.VMEM((total, 2 * rows), F32),
            pltpu.VMEM((heads, rows), F32),
            pltpu.VMEM((heads, rows), F32),
            pltpu.VMEM((per * count, rows), F32),
            pltpu.VMEM((per * count, rows), F32),
            pltpu.VMEM((hc * rows, dk), BF16),
            pltpu.VMEM((hc * rows, dv), BF16),
            pltpu.VMEM((total, hc * rows), BF16),
            pltpu.VMEM((total, hc * rows), BF16),
            pltpu.VMEM((win, dk), F32),
            pltpu.VMEM((win, dv), F32),
        ],
        input_output_aliases=aliases,
        cost_estimate=pl.CostEstimate(flops=4 * flops, bytes_accessed=rows * heads * (dk + dv) * 4, transcendentals=0),
        compiler_params=pltpu.CompilerParams(vmem_limit_bytes=VLIM),
    )(*args)


def finish_kernel(dims, cmp_ref, *refs):
    groups, dk, dv, off, halves = dims
    k_ref, v_ref = refs[-2:]
    ins = refs[:-2]
    kw = groups * dk
    each = groups // halves
    per_half = len(ins) // halves
    ks, vs = [], []
    for half in range(halves):
        mine = ins[half * per_half : (half + 1) * per_half]
        for g in range(each):
            total = mine[0][g]
            for ref in mine[1:]:
                total = total + ref[g].astype(F32)
            ks.append(total[:, :dk])
            vs.append(total[:, off:])
    k_ref[...] = (jnp.concatenate(ks, axis=1) + cmp_ref[:, :kw]).astype(BF16)
    v_ref[...] = (jnp.concatenate(vs, axis=1) + cmp_ref[:, kw:]).astype(BF16)


def finish(own_cmp, parts, groups, dk, dv, off, halves):
    rows = own_cmp.shape[0]
    return pl.pallas_call(
        functools.partial(finish_kernel, (groups, dk, dv, off, halves)),
        out_shape=(
            jax.ShapeDtypeStruct((rows, groups * dk), BF16),
            jax.ShapeDtypeStruct((rows, groups * dv), BF16),
        ),
        in_specs=[full()] * (1 + len(parts)),
        out_specs=(full(),) * 2,
        compiler_params=pltpu.CompilerParams(vmem_limit_bytes=VLIM),
    )(own_cmp, *parts)


def send_back(send, rows, reach):
    devices = lax.axis_size("seq")
    got = []
    for distance in range(1, reach + 1):
        at = (reach - distance) * rows
        pairs = [(i, i - distance) for i in range(devices) if i - distance >= 0]
        got.append(lax.ppermute(send[:, at : at + rows], "seq", pairs))
    return got


def on_device(queries, keys_in, values_in, gate_cmp, gate_win, cotangent, compress_key, compress_value):
    rows = queries.shape[1]
    dk, dv = compress_key.shape[1], compress_value.shape[1]
    groups = keys_in.shape[2] // dk
    devices = lax.axis_size("seq")
    reach = (WIN + rows - 1) // rows
    off = up128(dk)
    q, c = queries[0], cotangent[0]
    gc, gw = gate_cmp[0], gate_win[0]
    kv_all = gather_seq(keys_in[0], values_in[0])
    nb = kv_all.shape[0] // STRIDE
    prepped = prep(kv_all, compress_key, compress_value, groups, rows, reach)
    part = cmp_grads(q, c, prepped[0], prepped[2], gc, groups, reach, nb, off)
    total = sum_seq(part)
    gwk, gwv, own_cmp = back(total, kv_all, compress_key, compress_value, groups, rows, off, devices)
    kall, gwk, gwv = lax.optimization_barrier((prepped[0], gwk, gwv))
    gwk_sum, gwv_sum = lax.psum(gwk, "dp"), lax.psum(gwv, "dp")
    prepped = (kall, *prepped[1:])
    att, gq, send, own, ggc, ggw = attend(
        q, c, prepped, gc, gw, 0, groups, groups, reach, nb, off, None
    )
    send, gwk_sum, gwv_sum = lax.optimization_barrier((send, gwk_sum, gwv_sum))
    got = send_back(send, rows, reach)
    gk, gv = finish(own_cmp, [own, *got], groups, dk, dv, off, 1)
    return (
        att[None],
        gq[None],
        gk[None],
        gv[None],
        ggc[None],
        ggw[None],
        gwk_sum.astype(F32),
        gwv_sum.astype(F32),
    )


def solution(mesh):
    tokens = P("dp", "seq", None)
    in_specs = (tokens,) * 6 + (P(), P())
    out_specs = (tokens,) * 6 + (P("seq", None), P("seq", None))
    return jax.shard_map(on_device, mesh=mesh, in_specs=in_specs, out_specs=out_specs, check_vma=False)
```
